128 devices in a mesh: dp: 16 (over x, y), seq: 8 (over z, core).
Axes of the slice: x: 4, y: 4, z: 4, core: 2. Of those that a mesh axis runs over, the one named last changes fastest.
Arguments:
- queries: bfloat16 [16, 8, 512, 32, 128], P('dp', 'seq'), may hold values from -6 to 6
- key_rows: bfloat16 [16, 8, 512, 32, 128], P('dp', 'seq'), may hold values from -6 to 6
- value_rows: bfloat16 [16, 8, 512, 32, 128], P('dp', 'seq'), may hold values from -6 to 6
- destination: int32 [16, 8, 512], P('dp', 'seq'), may hold values from 0 to 15, as said below
- doc_starts: int32 [16, 8, 512], P('dp', 'seq'), may hold values 0 or 1
- decay_rate: float32 [32], replicated, may hold values from 3.8146973e-06 to 0.04
- norm_gain: float32 [32, 128], replicated, may hold values from 0.1 to 1.9
Outputs:
- attended: bfloat16 [16, 8, 512, 32, 128], P('dp', 'seq')
The draws below stay inside these ranges and needn't reach their ends.
Inputs may be any that keep to these rules, and one draw needn't show every extreme that they name: `destination`: each loader sends at most 48 of its rows to one sequence; at each seq index one sequence, drawn afresh, receives exactly 48 rows from every loader.
All inputs are finite; a program needn't handle non-finite values. No bound on the sum of `doc_starts` on one device may be relied on, other than what follows from the above.
Results may differ from the reference program's by a relative error of at most 0.0055.
Values may be sent and summed in bfloat16 or wider, within the bound.
No kernel may reach another device: no remote copies, remote signals or barrier semaphores. Data moves between devices by JAX's collectives and lax.ppermute only.
A program may use at most 192 MiB of HBM per device.

```python
import math
import jax
import jax.numpy as jnp
from jax import lax

H = 32
DH = 128
BLK = 384
TOK_DEV = 512
LOADERS = 16
SHARDS = 8
CAP = 48
CHAIN = 4096


def draw_destination(key, part):
    hot_key, row_key = jax.random.split(jax.random.fold_in(key, 11))
    hot_seq = jax.random.randint(hot_key, (SHARDS,), 0, LOADERS).astype(jnp.int32)
    hot_all = jnp.tile(hot_seq, LOADERS)
    row_keys = jax.random.split(row_key, LOADERS * SHARDS)

    def one_loader(loader_key, hot_target):
        pick_key, order_key = jax.random.split(loader_key)
        picks = jax.random.permutation(pick_key, (LOADERS - 1) * CAP)[:TOK_DEV - CAP].astype(jnp.int32)
        others = picks // CAP
        others = others + (others >= hot_target).astype(jnp.int32)
        targets = jnp.concatenate([jnp.full((CAP,), hot_target, jnp.int32), others.astype(jnp.int32)])
        order = jax.random.permutation(order_key, TOK_DEV).astype(jnp.int32)
        return targets[order]
    rows = jax.vmap(one_loader)(row_keys, hot_all)
    return rows.reshape(LOADERS, SHARDS, TOK_DEV).astype(jnp.int32)


def draw_decay_rate(key, part):
    uniform_part = jax.random.uniform(jax.random.fold_in(key, 23), (H,), jnp.float32)
    low_end = math.log(1.0 / (64.0 * CHAIN))
    high_end = math.log(1.0 / 25.0)
    return jnp.exp(low_end + (high_end - low_end) * uniform_part).astype(jnp.float32)


def touch_ends(result, rng, least, top_value):
    longest = result.shape.index(max(result.shape))
    spots = []
    for shift in (0, 1):
        where = [jax.random.randint(jax.random.fold_in(rng, axis), (), 0, length) for axis, length in enumerate(result.shape)]
        where[longest] = (where[longest] + shift) % result.shape[longest]
        spots.append(tuple(where))
    return result.at[spots[0]].set(least).at[spots[1]].set(top_value)


def level_of(rng, shape, cuts, smallest, high):
    level, own = 1.0, jax.random.fold_in(rng, 6)
    for dim, blocks in cuts:
        heights = jnp.exp(jax.random.uniform(jax.random.fold_in(own, dim), (blocks,), jnp.float32, smallest / len(cuts), high / len(cuts)))
        level = level * jnp.repeat(heights, shape[dim] // blocks).reshape([-1 if axis == dim else 1 for axis in range(len(shape))])
    return level


def gaussian(rng, shape, spread, reach, cuts=(), held_as=jnp.bfloat16):
    factor_of = level_of(rng, shape, cuts, -0.22, 0.18) if cuts else 1.0
    array = jax.random.normal(rng, shape, jnp.float32) * spread * factor_of
    return jnp.minimum(jnp.maximum(array, -reach), reach).astype(held_as)


def setup_inputs(seed: int = 0) -> dict:
    streams_of = jax.random.split(jax.random.key(seed), 8)
    return {
        "queries": gaussian(streams_of[0], (LOADERS, SHARDS, TOK_DEV, H, DH), 1.0, 6.0, ((0, 16), (1, 8))),
        "key_rows": gaussian(streams_of[1], (LOADERS, SHARDS, TOK_DEV, H, DH), 1.0, 6.0, ((0, 16), (1, 8))),
        "value_rows": gaussian(streams_of[2], (LOADERS, SHARDS, TOK_DEV, H, DH), 1.0, 6.0, ((0, 16), (1, 8))),
        "destination": draw_destination(jax.random.fold_in(streams_of[7], 71), 0),
        "doc_starts": touch_ends((jax.random.randint(streams_of[4], (LOADERS, SHARDS, TOK_DEV), 0, 4 * CHAIN) < 1).astype(jnp.int32), jax.random.fold_in(streams_of[4], 1), 0, 1),
        "decay_rate": draw_decay_rate(jax.random.fold_in(streams_of[7], 71), 0),
        "norm_gain": jnp.clip(1.0 + 0.18 * jax.random.normal(streams_of[6], (H, DH), jnp.float32), 0.1, 1.9),
    }


eps_norm = 1e-06

def to_half(values_in):
    return lax.optimization_barrier(values_in.astype(jnp.bfloat16)).astype(jnp.float32)

def attend_block(carry_state, block_inputs, decay_rate, norm_gain):
    block_query, block_key, block_value, block_count, block_doc, block_live, block_start = block_inputs
    before_count = block_count[0] - block_live[0]
    before_doc = block_doc[0] - block_start[0]
    positions = jnp.arange(BLK, dtype=jnp.int32)
    causal = positions[:, None] >= positions[None, :]
    same_doc = block_doc[:, None] == block_doc[None, :]
    keep_mask = causal & same_doc & (block_live[None, :] == 1)
    distance = jnp.maximum(block_count[:, None] - block_count[None, :], 0).astype(jnp.float32)
    weight = jnp.where(keep_mask[None], jnp.exp(-decay_rate[:, None, None] * distance[None]), 0.0)
    query_wide = block_query.astype(jnp.float32)
    key_wide = block_key.astype(jnp.float32)
    value_wide = block_value.astype(jnp.float32)
    scores = jnp.einsum('phd,qhd->hpq', query_wide, key_wide)
    weights_half = to_half(scores * weight)
    intra_term = jnp.einsum('hpq,qhd->phd', weights_half, value_wide)
    since = (block_count - before_count).astype(jnp.float32)
    carry_weight = jnp.where((block_doc == before_doc)[:, None], jnp.exp(-decay_rate[None, :] * since[:, None]), 0.0)
    state_half = to_half(carry_state)
    inter_term = jnp.einsum('phd,hde->phe', query_wide, state_half) * carry_weight[:, :, None]
    mixed_out = intra_term + inter_term
    end_count = block_count[-1]
    end_doc = block_doc[-1]
    until = (end_count - block_count).astype(jnp.float32)
    key_keep = (block_live == 1) & (block_doc == end_doc)
    key_weight = jnp.where(key_keep[:, None], jnp.exp(-decay_rate[None, :] * until[:, None]), 0.0)
    scaled_keys = to_half(key_wide * key_weight[:, :, None])
    update = jnp.einsum('phd,phe->hde', scaled_keys, value_wide)
    block_span = (end_count - before_count).astype(jnp.float32)
    block_decay = jnp.where(end_doc == before_doc, jnp.exp(-decay_rate * block_span), 0.0)
    new_state = block_decay[:, None, None] * carry_state + update
    mean_square = lax.optimization_barrier(jnp.mean(mixed_out * mixed_out, axis=(1, 2)))
    normed = (mixed_out * lax.rsqrt(mean_square + eps_norm)[:, None, None] * norm_gain[None]).astype(jnp.bfloat16)
    return (new_state, normed)

def attend_sequence(table_query, table_key, table_value, table_live, table_start, decay_rate, norm_gain):
    total = SHARDS * LOADERS * CAP
    live_flat = table_live.reshape(total)
    start_flat = table_start.reshape(total)
    live_count = jnp.cumsum(live_flat, dtype=jnp.int32)
    doc_count = jnp.cumsum(start_flat, dtype=jnp.int32)
    block_total = total // BLK

    def shaped(values_in):
        return values_in.reshape((block_total, BLK) + values_in.shape[3:])
    block_inputs = (shaped(table_query), shaped(table_key), shaped(table_value), live_count.reshape(block_total, BLK), doc_count.reshape(block_total, BLK), live_flat.reshape(block_total, BLK), start_flat.reshape(block_total, BLK))

    def advance(carry_state, inputs):
        return attend_block(carry_state, inputs, decay_rate, norm_gain)
    first_state = jnp.zeros((H, DH, DH), jnp.float32)
    final_state, normed = lax.scan(advance, first_state, block_inputs)
    return normed.reshape(SHARDS, LOADERS, CAP, H, DH)

def reference(queries, key_rows, value_rows, destination, doc_starts, decay_rate, norm_gain):
    targets = jnp.arange(LOADERS, dtype=jnp.int32)
    onehot = (destination[..., None] == targets).astype(jnp.int32)
    slot = lax.optimization_barrier(jnp.sum(jnp.cumsum(onehot, axis=2, dtype=jnp.int32) * onehot, axis=-1, dtype=jnp.int32)) - 1
    shard_ids = jnp.broadcast_to(jnp.arange(SHARDS, dtype=jnp.int32)[None, :, None], destination.shape)
    source_ids = jnp.broadcast_to(jnp.arange(LOADERS, dtype=jnp.int32)[:, None, None], destination.shape)
    slot_read = jnp.minimum(slot, CAP - 1).astype(jnp.int32)

    def one_sequence(output_acc, sequence_id):
        chosen = destination == sequence_id
        slot_write = jnp.where(chosen, slot, CAP).astype(jnp.int32)

        def table(values_in, dtype):
            empty = jnp.zeros((SHARDS, LOADERS, CAP) + values_in.shape[3:], dtype)
            return empty.at[shard_ids, source_ids, slot_write].set(values_in, mode='drop')
        table_query = table(queries, jnp.bfloat16)
        table_key = table(key_rows, jnp.bfloat16)
        table_value = table(value_rows, jnp.bfloat16)
        table_live = table(jnp.ones_like(destination), jnp.int32)
        table_start = table(doc_starts, jnp.int32)
        normed = attend_sequence(table_query, table_key, table_value, table_live, table_start, decay_rate, norm_gain)
        rows_back = normed[shard_ids, source_ids, slot_read]
        return (jnp.where(chosen[..., None, None], rows_back, output_acc), None)
    initial = jnp.zeros(queries.shape, jnp.bfloat16)
    attended, unused = lax.scan(one_sequence, initial, jnp.arange(LOADERS, dtype=jnp.int32))
    return attended
```

```python
import functools

import jax
import jax.numpy as jnp
from jax import lax
from jax.experimental import pallas as pl
from jax.experimental.pallas import tpu as pltpu
from jax.sharding import PartitionSpec as P

eps_norm = 1e-06
bf16 = jnp.bfloat16
f32 = jnp.float32
tiny = pl.CostEstimate(flops=1 << 20, bytes_accessed=1 << 16, transcendentals=0)


def params(mib, order):
    return pltpu.CompilerParams(vmem_limit_bytes=mib << 20, dimension_semantics=order)


def prepare_kernel(half, rate_ref, key_ref, value_ref, gap_ref, send_ref, turned_ref):
    heads = key_ref.shape[1]
    gap = gap_ref[...]
    keys = jnp.swapaxes(key_ref[...], 0, 1)
    turned_ref[...] = keys
    send_ref[:, 1] = jnp.swapaxes(value_ref[...], 0, 1)
    for h in range(heads):
        scale = jnp.where(gap >= 0.0, jnp.exp(gap * -rate_ref[half * heads + h]), 0.0)
        send_ref[h, 0] = (keys[h].astype(f32) * scale).astype(bf16)


def prepare(rate, keys, values, gap_wide, half):
    all_rows, all_heads, size = keys.shape
    heads = all_heads // 2
    rows = 64
    block = pl.BlockSpec((rows, heads, size), lambda i: (i, half, 0))
    return pl.pallas_call(
        functools.partial(prepare_kernel, half),
        grid=(all_rows // rows,),
        in_specs=[
            pl.BlockSpec(memory_space=pltpu.SMEM),
            block,
            block,
            pl.BlockSpec((rows, size), lambda i: (i, 0)),
        ],
        out_specs=[
            pl.BlockSpec((heads, 2, rows, size), lambda i: (0, 0, i, 0)),
            pl.BlockSpec((heads, rows, size), lambda i: (0, i, 0)),
        ],
        out_shape=[
            jax.ShapeDtypeStruct((heads, 2, all_rows, size), bf16),
            jax.ShapeDtypeStruct((heads, all_rows, size), bf16),
        ],
        compiler_params=params(32, ("arbitrary",)),
        cost_estimate=tiny,
        name="prepare",
    )(rate, keys, values, gap_wide)


def intra_kernel(first_ref, second_ref, k_ref, v_ref, col_ref, mask_ref, out_ref):
    part = first_ref.shape[2]
    for piece, q_ref in enumerate((first_ref, second_ref)):
        here = slice(piece * part, (piece + 1) * part)
        until = (piece + 1) * part
        scores = lax.dot_general(
            q_ref[0, 0], k_ref[0, :until], (((1,), (1,)), ((), ())), preferred_element_type=f32
        )
        weights = (scores * col_ref[0, :, :until] * mask_ref[here, :until]).astype(bf16)
        out_ref[0, here] = jnp.dot(weights, v_ref[0, 0, :until], preferred_element_type=f32)


def intra(query_parts, key_t, sent, col_scale, mask, half):
    heads, rows, size = key_t.shape
    shift = half * heads
    part = pl.BlockSpec((1, 1, rows // 2, size), lambda h: (h, half, 0, 0))
    return pl.pallas_call(
        intra_kernel,
        grid=(heads,),
        in_specs=[
            part,
            part,
            pl.BlockSpec((1, rows, size), lambda h: (h, 0, 0)),
            pl.BlockSpec((1, 1, rows, size), lambda h: (h, 1, 0, 0)),
            pl.BlockSpec((1, 1, rows), lambda h: (h + shift, 0, 0)),
            pl.BlockSpec((rows, rows), lambda h: (0, 0)),
        ],
        out_specs=pl.BlockSpec((1, rows, size), lambda h: (h, 0, 0)),
        out_shape=jax.ShapeDtypeStruct((heads, rows, size), f32),
        compiler_params=params(32, ("arbitrary",)),
        cost_estimate=tiny,
        name="intra",
    )(*query_parts, key_t, sent, col_scale, mask)


def update_kernel(decay_ref, pair_ref, dest_ref, prefix_ref, total_ref, spread):
    loader = pl.program_id(0)
    rows, size = pair_ref.shape[2:]
    sequences = total_ref.shape[0] // size

    @pl.when(loader == 0)
    def _():
        total_ref[...] = jnp.zeros_like(total_ref)

    dest = jnp.broadcast_to(dest_ref[0], (size, rows))
    key_turned = pair_ref[0, 0].T
    for g in range(sequences):
        spread[g * size : (g + 1) * size] = jnp.where(dest == g, key_turned, jnp.zeros_like(key_turned))
    update = jnp.dot(spread[...], pair_ref[0, 1], preferred_element_type=f32)
    for g in range(sequences):
        place = slice(g * size, (g + 1) * size)
        state = total_ref[place]
        prefix_ref[0, place] = state.astype(bf16)
        total_ref[place] = state * decay_ref[loader, g] + update[place]


def update_states(decay, pairs_in, dest_in):
    loaders, _, rows, size = pairs_in.shape
    sequences = decay.shape[1]
    wide = sequences * size
    return pl.pallas_call(
        update_kernel,
        grid=(loaders,),
        in_specs=[
            pl.BlockSpec(memory_space=pltpu.SMEM),
            pl.BlockSpec((1, 2, rows, size), lambda d: (d, 0, 0, 0)),
            pl.BlockSpec((1, 1, rows), lambda d: (d, 0, 0)),
        ],
        out_specs=[
            pl.BlockSpec((1, wide, size), lambda d: (d, 0, 0)),
            pl.BlockSpec((wide, size), lambda d: (0, 0)),
        ],
        out_shape=[
            jax.ShapeDtypeStruct((loaders, wide, size), bf16),
            jax.ShapeDtypeStruct((wide, size), f32),
        ],
        scratch_shapes=[pltpu.VMEM((wide, rows), bf16)],
        compiler_params=params(48, ("arbitrary",)),
        cost_estimate=tiny,
        name="update_states",
    )(decay, pairs_in, dest_in)


def inter_kernel(decay_ref, query_ref, dest_ref, prefix_ref, state_ref, *rest):
    out_ref, entry, spread = rest[-3:]
    loader = pl.program_id(0)
    size = query_ref.shape[3]
    sequences = state_ref.shape[0] // size
    dest = dest_ref[0]
    query = query_ref[0, 0]
    for g in range(sequences):
        place = slice(g * size, (g + 1) * size)
        entry[place] = (
            prefix_ref[0, place].astype(f32) + state_ref[place] * decay_ref[loader, g]
        ).astype(bf16)
        spread[:, place] = jnp.where(dest == g, query, jnp.zeros_like(query))
    out_ref[0, 0] = jnp.dot(spread[...], entry[...], preferred_element_type=f32).astype(bf16)


def inter(decay, query_in, dest_wide, prefix, state, piece, half, before):
    loaders, _, rows, size = query_in.shape
    wide = state.shape[0]
    block = pl.BlockSpec((1, 1, rows, size), lambda d: (d, half, 0, 0))
    extra = [] if before is None else [before]
    return pl.pallas_call(
        inter_kernel,
        grid=(loaders,),
        in_specs=[
            pl.BlockSpec(memory_space=pltpu.SMEM),
            block,
            pl.BlockSpec((1, rows, size), lambda d: (d, piece, 0)),
            pl.BlockSpec((1, wide, size), lambda d: (d, 0, 0)),
            pl.BlockSpec((wide, size), lambda d: (0, 0)),
        ]
        + [pl.BlockSpec(memory_space=pl.ANY)] * len(extra),
        out_specs=block,
        out_shape=jax.ShapeDtypeStruct(query_in.shape, bf16),
        scratch_shapes=[pltpu.VMEM((wide, size), bf16), pltpu.VMEM((rows, wide), bf16)],
        input_output_aliases={5: 0} if extra else {},
        compiler_params=params(48, ("arbitrary",)),
        cost_estimate=tiny,
        name="inter",
    )(decay, query_in, dest_wide, prefix, state, *extra)


def finish_kernel(rate_ref, inter_ref, low_ref, high_ref, slot_ref, keep_ref, gain_ref, *rest):
    out_ref, mixed = rest[-2:]
    heads, rows, size = low_ref.shape
    slot = slot_ref[...]
    keep = keep_ref[...]
    square = jnp.zeros((rows, size), f32)
    for half, intra_ref in enumerate((low_ref, high_ref)):
        for h in range(heads):
            rate = rate_ref[half * heads + h]
            value = jnp.exp(slot * -rate) * (intra_ref[h] + keep * inter_ref[h, half].astype(f32))
            mixed[half * heads + h] = value
            square = square + value * value
    mean_square = jnp.sum(square, axis=1, keepdims=True) / (2 * heads * size)
    factor = lax.rsqrt(mean_square + eps_norm)
    normed = (mixed[...] * factor[None]) * gain_ref[...]
    out_ref[...] = jnp.swapaxes(normed.astype(bf16), 0, 1)


def finish(rate, inter_back, intra_terms, slot_wide, keep_wide, gain, piece, pieces, before):
    heads, all_rows, size = intra_terms[0].shape
    part = all_rows // pieces
    rows = min(64, part)
    steps = part // rows
    shift = piece * steps
    extra = [] if before is None else [before]
    return pl.pallas_call(
        finish_kernel,
        grid=(steps,),
        in_specs=[
            pl.BlockSpec(memory_space=pltpu.SMEM),
            pl.BlockSpec((heads, 2, rows, size), lambda i: (0, 0, i, 0)),
            pl.BlockSpec((heads, rows, size), lambda i: (0, i + shift, 0)),
            pl.BlockSpec((heads, rows, size), lambda i: (0, i + shift, 0)),
            pl.BlockSpec((rows, size), lambda i: (i + shift, 0)),
            pl.BlockSpec((rows, size), lambda i: (i + shift, 0)),
            pl.BlockSpec((2 * heads, 1, size), lambda i: (0, 0, 0)),
        ]
        + [pl.BlockSpec(memory_space=pl.ANY)] * len(extra),
        out_specs=pl.BlockSpec((rows, 2 * heads, size), lambda i: (i + shift, 0, 0)),
        out_shape=jax.ShapeDtypeStruct((all_rows, 2 * heads, size), bf16),
        scratch_shapes=[pltpu.VMEM((2 * heads, rows, size), f32)],
        input_output_aliases={7: 0} if extra else {},
        compiler_params=params(48, ("arbitrary",)),
        cost_estimate=tiny,
        name="finish",
    )(rate, inter_back, *intra_terms, slot_wide, keep_wide, gain, *extra)


def swap(block, distance):
    count = lax.axis_size("seq")
    route = [(i, i + distance) for i in range(count) if i + distance < count]
    return lax.ppermute(block, "seq", route)


def other_core(block):
    return lax.ppermute(block, "seq", [(i, i ^ 1) for i in range(lax.axis_size("seq"))])


def incoming_states(total, shard_counts, shard_starts, rate):
    shards, all_sequences = shard_counts.shape
    sequences = all_sequences // 2
    shard = lax.axis_index("seq")
    core = shard % 2
    even = core == 0
    chip = shard // 2
    wide, size = total.shape
    part = wide // 2
    shard_ids = jnp.arange(shards, dtype=jnp.int32)
    counts_own = lax.dynamic_slice_in_dim(shard_counts, core * sequences, sequences, 1)
    starts_own = lax.dynamic_slice_in_dim(shard_starts, core * sequences, sequences, 1)

    def decay_of(first, last):
        inside = ((shard_ids >= first) & (shard_ids < last)).astype(f32)[:, None]
        count = jnp.sum(counts_own * inside, axis=0)
        starts = jnp.sum(starts_own * inside, axis=0)
        factor = jnp.where(starts == 0, jnp.exp(-rate * count), 0.0)
        return jnp.broadcast_to(factor[:, None, None], (sequences, size, 1)).reshape(part, 1)

    own = jnp.where(even, total[:part], total[part:])
    arrived = other_core(jnp.where(even, total[part:], total[:part]))
    total_even = jnp.where(even, own, arrived)
    total_odd = jnp.where(even, arrived, own)
    chip_half = (decay_of(2 * chip + 1, 2 * chip + 2) * total_even + total_odd).astype(bf16)
    base = jnp.zeros_like(total_even)
    for distance in range(1, shards // 2):
        earlier = swap(chip_half, 2 * distance).astype(f32)
        base = base + decay_of(2 * (chip - distance + 1), 2 * chip) * earlier
    later = decay_of(2 * chip, 2 * chip + 1) * base + total_even
    mine = jnp.where(even, base, later)
    got = other_core(jnp.where(even, later, base))
    return jnp.concatenate([jnp.where(even, mine, got), jnp.where(even, got, mine)])


def per_device(queries, key_rows, value_rows, destination, doc_starts, decay_rate, norm_gain):
    loaders = lax.axis_size("dp")
    rows, heads, size = queries.shape[2:]
    pieces = 2
    part = rows // pieces
    extra = 16
    lines = rows // size

    def exchange(block):
        return lax.all_to_all(block, "dp", split_axis=0, concat_axis=0, tiled=True)

    def after(block, *others):
        return lax.optimization_barrier((block,) + others)[0]

    dest = destination[0, 0]
    start = doc_starts[0, 0]
    sequence_ids = jnp.arange(loaders, dtype=jnp.int32)
    onehot = (dest[:, None] == sequence_ids[None, :]).astype(jnp.int32)
    both = jnp.concatenate([onehot, onehot * start[:, None]], axis=1)
    row_ids = jnp.arange(rows, dtype=jnp.int32)
    causal = row_ids[:, None] >= row_ids[None, :]
    summed = jnp.dot(causal.astype(bf16), both.astype(bf16), preferred_element_type=f32)

    info = jnp.concatenate(
        [
            dest.astype(bf16).reshape(lines, size),
            jnp.pad(summed[-1:].astype(bf16), ((0, extra - lines - 1), (0, size - 2 * loaders))),
        ]
    )
    info_all = exchange(jnp.broadcast_to(info[None], (loaders, extra, size)))

    onehot_f = onehot.astype(f32)
    counts = summed[:, :loaders]
    docs = summed[:, loaders:]
    slot = jnp.sum(counts * onehot_f, axis=1)
    doc = jnp.sum(docs * onehot_f, axis=1)
    last_count = jnp.sum(counts[-1:] * onehot_f, axis=1)
    last_doc = jnp.sum(docs[-1:] * onehot_f, axis=1)
    gap = jnp.where(doc == last_doc, last_count - slot, -1.0)
    gap_wide = jnp.broadcast_to(gap[:, None], (rows, size))

    sent, keys_t = [], []
    for half in range(2):
        send, key_t = prepare(decay_rate, key_rows[0, 0], value_rows[0, 0], gap_wide, half)
        sent.append(send)
        keys_t.append(key_t)
    pairs_in = [exchange(after(sent[0], info_all))]

    query_parts = [
        jnp.transpose(
            queries[0, 0, i * part : (i + 1) * part].reshape(part, 2, loaders, size), (2, 1, 0, 3)
        )
        for i in range(pieces)
    ]
    label = dest * rows + doc.astype(jnp.int32)
    mask = (causal & (label[:, None] == label[None, :])).astype(f32)
    col_scale = jnp.exp(decay_rate[:, None] * slot[None])[:, None]
    intra_terms = [
        intra(query_parts, keys_t[half], sent[half], col_scale, mask, half) for half in range(2)
    ]
    slot_wide = jnp.broadcast_to(slot[:, None], (rows, size))
    keep_wide = jnp.broadcast_to((doc == 0).astype(f32)[:, None], (rows, size))

    dest_all = info_all[:, :lines].reshape(loaders, rows)
    count_all = info_all[:, lines, :loaders].astype(f32)
    start_all = info_all[:, lines, loaders : 2 * loaders].astype(f32)
    dest_wide = jnp.broadcast_to(dest_all[:, :, None], (loaders, rows, size))
    shard_info = jnp.concatenate([jnp.sum(count_all, axis=0), jnp.sum(start_all, axis=0)])
    shard_all = lax.all_gather(shard_info, "seq", axis=0, tiled=False)
    shard_counts = shard_all[:, :loaders]
    shard_starts = shard_all[:, loaders:]
    place = lax.axis_index("dp")
    rates = [decay_rate[place], decay_rate[loaders + place]]
    earlier = (sequence_ids[:, None] > sequence_ids[None, :]).astype(f32)[:, :, None]
    count_before = jnp.sum(earlier * count_all[None], axis=1)
    start_before = jnp.sum(earlier * start_all[None], axis=1)
    chunk_decays = [jnp.where(start_all == 0, jnp.exp(-rate * count_all), 0.0) for rate in rates]
    entry_decays = [jnp.where(start_before == 0, jnp.exp(-rate * count_before), 0.0) for rate in rates]

    ready = (*intra_terms, slot_wide, keep_wide, dest_wide, shard_all, *chunk_decays, *entry_decays)
    pairs_in.append(exchange(after(sent[1], pairs_in[0], *ready)))

    queries_in = []
    before = pairs_in[1]
    prefixes, states = [], []
    for half in range(2):
        prefix, total = update_states(chunk_decays[half], pairs_in[half], dest_all[:, None])
        prefixes.append(prefix)
        states.append(incoming_states(total, shard_counts, shard_starts, rates[half]))
    before = (pairs_in[1], states[0])
    for i in range(pieces):
        queries_in.append(exchange(after(query_parts[i], *before)))
        before = (queries_in[-1],)

    backs = []
    for i in range(pieces):
        out = None
        for half in range(2):
            out = inter(
                entry_decays[half], queries_in[i], dest_wide, prefixes[half], states[half], i, half, out
            )
        backs.append(exchange(out))
    result = None
    gain = norm_gain[:, None]
    for i in range(pieces):
        result = finish(
            decay_rate, backs[i], intra_terms, slot_wide, keep_wide, gain, i, pieces, result
        )
    return result[None, None]


def solution(mesh):
    placed = (
        P("dp", "seq", None, None, None),
        P("dp", "seq", None, None, None),
        P("dp", "seq", None, None, None),
        P("dp", "seq", None),
        P("dp", "seq", None),
        P(),
        P(),
    )
    return jax.shard_map(
        per_device,
        mesh=mesh,
        in_specs=placed,
        out_specs=P("dp", "seq", None, None, None),
        check_vma=False,
    )
```

```python
import functools

import jax
import jax.numpy as jnp
from jax import lax
from jax.experimental import pallas as pl
from jax.experimental.pallas import tpu as pltpu
from jax.sharding import PartitionSpec as P

eps_norm = 1e-06
bf16 = jnp.bfloat16
f32 = jnp.float32
tiny = pl.CostEstimate(flops=1 << 20, bytes_accessed=1 << 16, transcendentals=0)


def params(mib, order):
    return pltpu.CompilerParams(vmem_limit_bytes=mib << 20, dimension_semantics=order)


def prepare_kernel(half, extra, rate_ref, key_ref, value_ref, gap_ref, *rest):
    send_ref, turned_ref = rest[-2:]
    rows, heads, size = key_ref.shape
    gap = gap_ref[...]
    keys = jnp.swapaxes(key_ref[...], 0, 1)
    turned_ref[...] = keys
    send_ref[:, 1] = jnp.swapaxes(value_ref[...], 0, 1)
    for h in range(heads):
        scale = jnp.where(gap >= 0.0, jnp.exp(gap * -rate_ref[half * heads + h]), 0.0)
        send_ref[h, 0] = (keys[h].astype(f32) * scale).astype(bf16)
    if extra:

        @pl.when(pl.program_id(0) == pl.num_programs(0) - 1)
        def _():
            send_ref[:, :, rows - extra :] = jnp.broadcast_to(
                rest[0][...][None, None], (heads, 2, extra, size)
            )


def prepare(rate, keys, values, gap_wide, half, info):
    all_rows, all_heads, size = keys.shape
    heads = all_heads // 2
    tail = [] if info is None else [info]
    extra = 0 if info is None else info.shape[0]
    steps = 3 if extra else 4
    rows = (all_rows + extra) // steps
    block = pl.BlockSpec((rows, heads, size), lambda i: (i, half, 0))
    return pl.pallas_call(
        functools.partial(prepare_kernel, half, extra),
        grid=(steps,),
        in_specs=[
            pl.BlockSpec(memory_space=pltpu.SMEM),
            block,
            block,
            pl.BlockSpec((rows, size), lambda i: (i, 0)),
        ]
        + [pl.BlockSpec((extra, size), lambda i: (0, 0))] * len(tail),
        out_specs=[
            pl.BlockSpec((heads, 2, rows, size), lambda i: (0, 0, i, 0)),
            pl.BlockSpec((heads, rows, size), lambda i: (0, i, 0)),
        ],
        out_shape=[
            jax.ShapeDtypeStruct((heads, 2, all_rows + extra, size), bf16),
            jax.ShapeDtypeStruct((heads, all_rows, size), bf16),
        ],
        compiler_params=params(60, ("arbitrary",)),
        cost_estimate=tiny,
        name="prepare",
    )(rate, keys, values, gap_wide, *tail)


def intra_kernel(base, rate_ref, q_ref, k_ref, v_ref, col_ref, mask_ref, slot_ref, out_ref):
    rate = rate_ref[base + pl.program_id(0)]
    part = k_ref.shape[1] // 2
    for piece in range(2):
        here = slice(piece * part, (piece + 1) * part)
        until = (piece + 1) * part
        scores = lax.dot_general(
            q_ref[0, 0, here], k_ref[0, :until], (((1,), (1,)), ((), ())), preferred_element_type=f32
        )
        weights = (scores * col_ref[0, :, :until] * mask_ref[here, :until]).astype(bf16)
        out_ref[0, here] = jnp.exp(slot_ref[here] * -rate) * jnp.dot(
            weights, v_ref[0, 0, :until], preferred_element_type=f32
        )


def intra(rate, queries, key_t, sent, col_scale, mask, slot_wide, half):
    heads, rows, size = key_t.shape
    shift = half * heads
    return pl.pallas_call(
        functools.partial(intra_kernel, shift),
        grid=(heads,),
        in_specs=[
            pl.BlockSpec(memory_space=pltpu.SMEM),
            pl.BlockSpec((1, 1, rows, size), lambda h: (h, 0, 0, 0)),
            pl.BlockSpec((1, rows, size), lambda h: (h, 0, 0)),
            pl.BlockSpec((1, 1, rows, size), lambda h: (h, 1, 0, 0)),
            pl.BlockSpec((1, 1, rows), lambda h: (h + shift, 0, 0)),
            pl.BlockSpec((rows, rows), lambda h: (0, 0)),
            pl.BlockSpec((rows, size), lambda h: (0, 0)),
        ],
        out_specs=pl.BlockSpec((1, rows, size), lambda h: (h, 0, 0)),
        out_shape=jax.ShapeDtypeStruct((heads, rows, size), f32),
        compiler_params=params(56, ("arbitrary",)),
        cost_estimate=tiny,
        name="intra",
    )(rate, queries, key_t, sent, col_scale, mask, slot_wide)


def update_kernel(decay_ref, pair_ref, dest_ref, prefix_ref, total_ref, spread):
    step = pl.program_id(0)
    group, _, rows, size = pair_ref.shape
    sequences = total_ref.shape[0] // size

    @pl.when(step == 0)
    def _():
        total_ref[...] = jnp.zeros_like(total_ref)

    for u in range(group):
        dest = jnp.broadcast_to(dest_ref[u], (size, rows))
        key_turned = pair_ref[u, 0].T
        for g in range(sequences):
            spread[u, g * size : (g + 1) * size] = jnp.where(
                dest == g, key_turned, jnp.zeros_like(key_turned)
            )
        update = jnp.dot(spread[u], pair_ref[u, 1], preferred_element_type=f32)
        for g in range(sequences):
            place = slice(g * size, (g + 1) * size)
            state = total_ref[place]
            prefix_ref[u, place] = state.astype(bf16)
            total_ref[place] = state * decay_ref[step * group + u, g] + update[place]


def update_states(decay, pairs_in, dest_in):
    loaders, _, _, size = pairs_in.shape
    rows = dest_in.shape[2]
    sequences = decay.shape[1]
    wide = sequences * size
    group = 2
    return pl.pallas_call(
        update_kernel,
        grid=(loaders // group,),
        in_specs=[
            pl.BlockSpec(memory_space=pltpu.SMEM),
            pl.BlockSpec((group, 2, rows, size), lambda d: (d, 0, 0, 0)),
            pl.BlockSpec((group, 1, rows), lambda d: (d, 0, 0)),
        ],
        out_specs=[
            pl.BlockSpec((group, wide, size), lambda d: (d, 0, 0)),
            pl.BlockSpec((wide, size), lambda d: (0, 0)),
        ],
        out_shape=[
            jax.ShapeDtypeStruct((loaders, wide, size), bf16),
            jax.ShapeDtypeStruct((wide, size), f32),
        ],
        scratch_shapes=[pltpu.VMEM((group, wide, rows), bf16)],
        compiler_params=params(48, ("arbitrary",)),
        cost_estimate=tiny,
        name="update_states",
    )(decay, pairs_in, dest_in)


def inter_kernel(rate_ref, decay_ref, query_ref, dest_ref, slot_ref, prefix_ref, state_ref, out_ref, entry, spread):
    step = pl.program_id(0)
    group, _, _, size = query_ref.shape
    sequences = state_ref.shape[0] // size
    rate = rate_ref[0]
    for u in range(group):
        dest = dest_ref[u]
        query = query_ref[u, 0]
        for g in range(sequences):
            place = slice(g * size, (g + 1) * size)
            entry[u, place] = (
                prefix_ref[u, place].astype(f32) + state_ref[place] * decay_ref[step * group + u, g]
            ).astype(bf16)
            spread[u, :, place] = jnp.where(dest == g, query, jnp.zeros_like(query))
        slot = slot_ref[u].astype(f32)
        factor = jnp.where(slot > 0.0, jnp.exp(slot * -rate), 0.0)
        product = jnp.dot(spread[u], entry[u], preferred_element_type=f32)
        out_ref[u] = (product * factor).astype(bf16)


def inter(rate, decay, query_in, dest_wide, slot_wide, prefix, state):
    loaders, rows, size = dest_wide.shape
    wide = state.shape[0]
    group = 2
    return pl.pallas_call(
        inter_kernel,
        grid=(loaders // group,),
        in_specs=[
            pl.BlockSpec(memory_space=pltpu.SMEM),
            pl.BlockSpec(memory_space=pltpu.SMEM),
            pl.BlockSpec((group, 1, rows, size), lambda d: (d, 0, 0, 0)),
            pl.BlockSpec((group, rows, size), lambda d: (d, 0, 0)),
            pl.BlockSpec((group, rows, size), lambda d: (d, 0, 0)),
            pl.BlockSpec((group, wide, size), lambda d: (d, 0, 0)),
            pl.BlockSpec((wide, size), lambda d: (0, 0)),
        ],
        out_specs=pl.BlockSpec((group, rows, size), lambda d: (d, 0, 0)),
        out_shape=jax.ShapeDtypeStruct((loaders, rows, size), bf16),
        scratch_shapes=[pltpu.VMEM((group, wide, size), bf16), pltpu.VMEM((group, rows, wide), bf16)],
        compiler_params=params(48, ("arbitrary",)),
        cost_estimate=tiny,
        name="inter",
    )(rate.reshape(1), decay, query_in, dest_wide, slot_wide, prefix, state)


def finish_kernel(inter_low, inter_high, intra_low, intra_high, gain_ref, out_ref, mixed):
    heads, rows, size = intra_low.shape
    square = jnp.zeros((rows, size), f32)
    for half, (inter_ref, intra_ref) in enumerate(((inter_low, intra_low), (inter_high, intra_high))):
        for h in range(heads):
            value = intra_ref[h] + inter_ref[h].astype(f32)
            mixed[half * heads + h] = value
            square = square + value * value
    mean_square = jnp.sum(square, axis=1, keepdims=True) / (2 * heads * size)
    factor = lax.rsqrt(mean_square + eps_norm)
    normed = (mixed[...] * factor[None]) * gain_ref[...]
    out_ref[...] = jnp.swapaxes(normed.astype(bf16), 0, 1)


def finish(inter_backs, intra_terms, gain):
    heads, all_rows, size = intra_terms[0].shape
    rows = 64
    block = pl.BlockSpec((heads, rows, size), lambda i: (0, i, 0))
    return pl.pallas_call(
        finish_kernel,
        grid=(all_rows // rows,),
        in_specs=[block] * 4 + [pl.BlockSpec((2 * heads, 1, size), lambda i: (0, 0, 0))],
        out_specs=pl.BlockSpec((rows, 2 * heads, size), lambda i: (i, 0, 0)),
        out_shape=jax.ShapeDtypeStruct((all_rows, 2 * heads, size), bf16),
        scratch_shapes=[pltpu.VMEM((2 * heads, rows, size), f32)],
        compiler_params=params(40, ("arbitrary",)),
        cost_estimate=tiny,
        name="finish",
    )(*inter_backs, *intra_terms, gain)


def swap(block, distance):
    count = lax.axis_size("seq")
    route = [(i, i + distance) for i in range(count) if i + distance < count]
    return lax.ppermute(block, "seq", route)


def other_core(block):
    return lax.ppermute(block, "seq", [(i, i ^ 1) for i in range(lax.axis_size("seq"))])


def incoming_states(total, counts, starts, rate):
    all_sequences = counts.shape[0]
    sequences = all_sequences // 2
    shard = lax.axis_index("seq")
    even = shard % 2 == 0
    wide, size = total.shape
    part = wide // 2
    chips = lax.axis_size("seq") // 2

    def decay(count, start):
        factor = jnp.where(start == 0.0, jnp.exp(-rate * count), 0.0)
        return jnp.broadcast_to(factor[:, None, None], (sequences, size, 1)).reshape(part, 1)

    def halves(numbers):
        return numbers[:sequences], numbers[sequences:]

    def lines(numbers, height, dtype):
        row = jnp.concatenate(numbers)
        row = jnp.pad(row, (0, size - row.shape[0]))
        return jnp.pad(row[None], ((0, height - 1), (0, 0))).astype(dtype)

    own = jnp.where(even, total[:part], total[part:])
    theirs = jnp.where(even, total[part:], total[:part])
    arrived = other_core(jnp.concatenate([theirs, lines([counts, starts], 8, f32)]))
    total_even = jnp.where(even, own, arrived[:part])
    total_odd = jnp.where(even, arrived[:part], own)
    facts = arrived[part]
    counts_low, counts_high = halves(counts)
    starts_low, starts_high = halves(starts)
    other_low, other_high = halves(facts[:all_sequences])
    begun_low, begun_high = halves(facts[all_sequences : 2 * all_sequences])
    counts_own = jnp.where(even, counts_low, counts_high)
    starts_own = jnp.where(even, starts_low, starts_high)
    counts_other = jnp.where(even, other_low, other_high)
    starts_other = jnp.where(even, begun_low, begun_high)
    decay_even = decay(jnp.where(even, counts_own, counts_other), jnp.where(even, starts_own, starts_other))
    decay_odd = decay(jnp.where(even, counts_other, counts_own), jnp.where(even, starts_other, starts_own))

    chip_count = counts_own + counts_other
    chip_start = jnp.minimum(starts_own + starts_other, 1.0)
    high = jnp.floor(chip_count / 128.0)
    packed = jnp.concatenate(
        [
            (decay_odd * total_even + total_odd).astype(bf16),
            lines([high, chip_count - 128.0 * high, chip_start], 16, bf16),
        ]
    )
    base = jnp.zeros_like(total_even)
    passed_count = jnp.zeros_like(chip_count)
    passed_start = jnp.zeros_like(chip_start)
    for distance in range(1, chips):
        earlier = swap(packed, 2 * distance)
        base = base + decay(passed_count, passed_start) * earlier[:part].astype(f32)
        row = earlier[part].astype(f32)
        passed_count = passed_count + 128.0 * row[:sequences] + row[sequences : 2 * sequences]
        passed_start = passed_start + row[2 * sequences : 3 * sequences]
    later = decay_even * base + total_even
    mine = jnp.where(even, base, later)
    got = other_core(jnp.where(even, later, base))
    return jnp.concatenate([jnp.where(even, mine, got), jnp.where(even, got, mine)])


def per_device(queries, key_rows, value_rows, destination, doc_starts, decay_rate, norm_gain):
    loaders = lax.axis_size("dp")
    rows, heads, size = queries.shape[2:]
    extra = 16
    lines = rows // size

    def exchange(block):
        return lax.all_to_all(block, "dp", split_axis=0, concat_axis=0, tiled=True)

    def after(block, *others):
        return lax.optimization_barrier((block,) + others)[0]

    dest = destination[0, 0]
    start = doc_starts[0, 0]
    sequence_ids = jnp.arange(loaders, dtype=jnp.int32)
    onehot = (dest[:, None] == sequence_ids[None, :]).astype(jnp.int32)
    both = jnp.concatenate([onehot, onehot * start[:, None]], axis=1)
    row_ids = jnp.arange(rows, dtype=jnp.int32)
    causal = row_ids[:, None] >= row_ids[None, :]
    summed = jnp.dot(causal.astype(bf16), both.astype(bf16), preferred_element_type=f32)

    onehot_f = onehot.astype(f32)
    counts = summed[:, :loaders]
    docs = summed[:, loaders:]
    slot = jnp.sum(counts * onehot_f, axis=1)
    doc = jnp.sum(docs * onehot_f, axis=1)
    last_count = jnp.sum(counts[-1:] * onehot_f, axis=1)
    last_doc = jnp.sum(docs[-1:] * onehot_f, axis=1)
    gap = jnp.where(doc == last_doc, last_count - slot, -1.0)
    gap_wide = jnp.broadcast_to(gap[:, None], (rows, size))
    info = jnp.concatenate(
        [
            dest.astype(bf16).reshape(lines, size),
            jnp.where(doc == 0, slot, 0.0).astype(bf16).reshape(lines, size),
            jnp.pad(summed[-1:].astype(bf16), ((0, extra - 2 * lines - 1), (0, size - 2 * loaders))),
        ]
    )

    keys_here, values_here = key_rows[0, 0], value_rows[0, 0]
    sent, keys_t, queries_t = [], [], []
    for half in range(2):
        send, key_t = prepare(decay_rate, keys_here, values_here, gap_wide, half, None if half else info)
        sent.append(send)
        keys_t.append(key_t)
        here = slice(half * loaders, (half + 1) * loaders)
        queries_t.append(jnp.transpose(queries[0, 0, :, here], (1, 0, 2))[:, None])
    first_in = exchange(sent[0])

    label = dest * rows + doc.astype(jnp.int32)
    mask = (causal & (label[:, None] == label[None, :])).astype(f32)
    col_scale = jnp.exp(decay_rate[:, None] * slot[None])[:, None]
    slot_here = jnp.broadcast_to(slot[:, None], (rows, size))
    intra_terms = [
        intra(decay_rate, queries_t[half], keys_t[half], sent[half], col_scale, mask, slot_here, half)
        for half in range(2)
    ]
    first_query = exchange(after(queries_t[0], first_in, *intra_terms))

    info_all = first_in[:, 0, rows:]
    dest_all = info_all[:, :lines].reshape(loaders, rows)
    slot_all = info_all[:, lines : 2 * lines].reshape(loaders, rows)
    count_all = info_all[:, 2 * lines, :loaders].astype(f32)
    start_all = info_all[:, 2 * lines, loaders : 2 * loaders].astype(f32)
    dest_wide = jnp.broadcast_to(dest_all[:, :, None], (loaders, rows, size))
    slot_wide = jnp.broadcast_to(slot_all[:, :, None], (loaders, rows, size))
    place = lax.axis_index("dp")
    rates = [decay_rate[place], decay_rate[loaders + place]]
    shard_counts = jnp.sum(count_all, axis=0)
    shard_starts = jnp.sum(start_all, axis=0)
    earlier = (sequence_ids[:, None] > sequence_ids[None, :]).astype(f32)[:, :, None]
    count_before = jnp.sum(earlier * count_all[None], axis=1)
    start_before = jnp.sum(earlier * start_all[None], axis=1)
    chunk_decays = [jnp.where(start_all == 0, jnp.exp(-rate * count_all), 0.0) for rate in rates]
    entry_decays = [jnp.where(start_before == 0, jnp.exp(-rate * count_before), 0.0) for rate in rates]

    prefix, total = update_states(chunk_decays[0], first_in, dest_all[:, None])
    second_in = exchange(after(sent[1], first_query, total))
    state = incoming_states(total, shard_counts, shard_starts, rates[0])
    low = inter(rates[0], entry_decays[0], first_query, dest_wide, slot_wide, prefix, state)

    second_in = after(second_in, low)
    second_query = exchange(after(queries_t[1], second_in))
    prefix, total = update_states(chunk_decays[1], second_in, dest_all[:, None])
    low_back = exchange(after(low, second_query))
    state = incoming_states(after(total, second_query), shard_counts, shard_starts, rates[1])
    high = inter(rates[1], entry_decays[1], second_query, dest_wide, slot_wide, prefix, state)
    high_back = exchange(after(high, low_back))
    result = finish((low_back, high_back), intra_terms, norm_gain[:, None])
    return result[None, None]


def solution(mesh):
    placed = (
        P("dp", "seq", None, None, None),
        P("dp", "seq", None, None, None),
        P("dp", "seq", None, None, None),
        P("dp", "seq", None),
        P("dp", "seq", None),
        P(),
        P(),
    )
    return jax.shard_map(
        per_device,
        mesh=mesh,
        in_specs=placed,
        out_specs=P("dp", "seq", None, None, None),
        check_vma=False,
    )
```

```python
import functools

import jax
import jax.numpy as jnp
from jax import lax
from jax.experimental import pallas as pl
from jax.experimental.pallas import tpu as pltpu
from jax.sharding import PartitionSpec as P

eps_norm = 1e-06
bf16 = jnp.bfloat16
f32 = jnp.float32
tiny = pl.CostEstimate(flops=1 << 20, bytes_accessed=1 << 16, transcendentals=0)


def params(mib, order):
    return pltpu.CompilerParams(vmem_limit_bytes=mib << 20, dimension_semantics=order)


def prepare_kernel(half, extra, rate_ref, key_ref, value_ref, gap_ref, *rest):
    send_ref, turned_ref = rest[-2:]
    rows, heads, size = key_ref.shape
    gap = gap_ref[...]
    keys = jnp.swapaxes(key_ref[...], 0, 1)
    turned_ref[...] = keys
    send_ref[:, 1] = jnp.swapaxes(value_ref[...], 0, 1)
    for h in range(heads):
        scale = jnp.where(gap >= 0.0, jnp.exp(gap * -rate_ref[half * heads + h]), 0.0)
        send_ref[h, 0] = (keys[h].astype(f32) * scale).astype(bf16)
    if extra:

        @pl.when(pl.program_id(0) == pl.num_programs(0) - 1)
        def _():
            send_ref[:, :, rows - extra :] = jnp.broadcast_to(
                rest[0][...][None, None], (heads, 2, extra, size)
            )


def prepare(rate, keys, values, gap_wide, half, info):
    all_rows, all_heads, size = keys.shape
    heads = all_heads // 2
    tail = [] if info is None else [info]
    extra = 0 if info is None else info.shape[0]
    steps = 3 if extra else 4
    rows = (all_rows + extra) // steps
    block = pl.BlockSpec((rows, heads, size), lambda i: (i, half, 0))
    return pl.pallas_call(
        functools.partial(prepare_kernel, half, extra),
        grid=(steps,),
        in_specs=[
            pl.BlockSpec(memory_space=pltpu.SMEM),
            block,
            block,
            pl.BlockSpec((rows, size), lambda i: (i, 0)),
        ]
        + [pl.BlockSpec((extra, size), lambda i: (0, 0))] * len(tail),
        out_specs=[
            pl.BlockSpec((heads, 2, rows, size), lambda i: (0, 0, i, 0)),
            pl.BlockSpec((heads, rows, size), lambda i: (0, i, 0)),
        ],
        out_shape=[
            jax.ShapeDtypeStruct((heads, 2, all_rows + extra, size), bf16),
            jax.ShapeDtypeStruct((heads, all_rows, size), bf16),
        ],
        compiler_params=params(60, ("arbitrary",)),
        cost_estimate=tiny,
        name="prepare",
    )(rate, keys, values, gap_wide, *tail)


def intra_kernel(base, rate_ref, q_ref, k_ref, v_ref, col_ref, mask_ref, slot_ref, out_ref):
    rate = rate_ref[base + pl.program_id(0)]
    part = k_ref.shape[1] // 2
    for piece in range(2):
        here = slice(piece * part, (piece + 1) * part)
        until = (piece + 1) * part
        scores = lax.dot_general(
            q_ref[0, 0, here], k_ref[0, :until], (((1,), (1,)), ((), ())), preferred_element_type=f32
        )
        weights = (scores * col_ref[0, :, :until] * mask_ref[here, :until]).astype(bf16)
        out_ref[0, here] = jnp.exp(slot_ref[here] * -rate) * jnp.dot(
            weights, v_ref[0, 0, :until], preferred_element_type=f32
        )


def intra(rate, queries, key_t, sent, col_scale, mask, slot_wide, half):
    heads, rows, size = key_t.shape
    shift = half * heads
    return pl.pallas_call(
        functools.partial(intra_kernel, shift),
        grid=(heads,),
        in_specs=[
            pl.BlockSpec(memory_space=pltpu.SMEM),
            pl.BlockSpec((1, 1, rows, size), lambda h: (h, 0, 0, 0)),
            pl.BlockSpec((1, rows, size), lambda h: (h, 0, 0)),
            pl.BlockSpec((1, 1, rows, size), lambda h: (h, 1, 0, 0)),
            pl.BlockSpec((1, 1, rows), lambda h: (h + shift, 0, 0)),
            pl.BlockSpec((rows, rows), lambda h: (0, 0)),
            pl.BlockSpec((rows, size), lambda h: (0, 0)),
        ],
        out_specs=pl.BlockSpec((1, rows, size), lambda h: (h, 0, 0)),
        out_shape=jax.ShapeDtypeStruct((heads, rows, size), f32),
        compiler_params=params(56, ("arbitrary",)),
        cost_estimate=tiny,
        name="intra",
    )(rate, queries, key_t, sent, col_scale, mask, slot_wide)


def update_kernel(decay_ref, pair_ref, dest_ref, prefix_ref, total_ref, spread):
    step = pl.program_id(0)
    group, _, rows, size = pair_ref.shape
    sequences = total_ref.shape[0] // size

    @pl.when(step == 0)
    def _():
        total_ref[...] = jnp.zeros_like(total_ref)

    for u in range(group):
        dest = jnp.broadcast_to(dest_ref[u], (size, rows))
        key_turned = pair_ref[u, 0].T
        for g in range(sequences):
            spread[u, g * size : (g + 1) * size] = jnp.where(
                dest == g, key_turned, jnp.zeros_like(key_turned)
            )
        update = jnp.dot(spread[u], pair_ref[u, 1], preferred_element_type=f32)
        for g in range(sequences):
            place = slice(g * size, (g + 1) * size)
            state = total_ref[place]
            prefix_ref[u, place] = state.astype(bf16)
            total_ref[place] = state * decay_ref[step * group + u, g] + update[place]


def update_states(decay, pairs_in, dest_in):
    loaders, _, _, size = pairs_in.shape
    rows = dest_in.shape[2]
    sequences = decay.shape[1]
    wide = sequences * size
    group = 2
    return pl.pallas_call(
        update_kernel,
        grid=(loaders // group,),
        in_specs=[
            pl.BlockSpec(memory_space=pltpu.SMEM),
            pl.BlockSpec((group, 2, rows, size), lambda d: (d, 0, 0, 0)),
            pl.BlockSpec((group, 1, rows), lambda d: (d, 0, 0)),
        ],
        out_specs=[
            pl.BlockSpec((group, wide, size), lambda d: (d, 0, 0)),
            pl.BlockSpec((wide, size), lambda d: (0, 0)),
        ],
        out_shape=[
            jax.ShapeDtypeStruct((loaders, wide, size), bf16),
            jax.ShapeDtypeStruct((wide, size), f32),
        ],
        scratch_shapes=[pltpu.VMEM((group, wide, rows), bf16)],
        compiler_params=params(48, ("arbitrary",)),
        cost_estimate=tiny,
        name="update_states",
    )(decay, pairs_in, dest_in)


def inter_kernel(rate_ref, decay_ref, query_ref, dest_ref, slot_ref, prefix_ref, state_ref, out_ref, entry, spread):
    step = pl.program_id(0)
    group, _, _, size = query_ref.shape
    sequences = state_ref.shape[0] // size
    rate = rate_ref[0]
    for u in range(group):
        dest = dest_ref[u]
        query = query_ref[u, 0]
        for g in range(sequences):
            place = slice(g * size, (g + 1) * size)
            entry[u, place] = (
                prefix_ref[u, place].astype(f32) + state_ref[place] * decay_ref[step * group + u, g]
            ).astype(bf16)
            spread[u, :, place] = jnp.where(dest == g, query, jnp.zeros_like(query))
        slot = slot_ref[u].astype(f32)
        factor = jnp.where(slot > 0.0, jnp.exp(slot * -rate), 0.0)
        product = jnp.dot(spread[u], entry[u], preferred_element_type=f32)
        out_ref[u] = (product * factor).astype(bf16)


def inter(rate, decay, query_in, dest_wide, slot_wide, prefix, state, piece, pieces):
    loaders, all_rows, size = dest_wide.shape
    rows = all_rows // pieces
    wide = state.shape[0]
    group = 2 * pieces
    block = pl.BlockSpec((group, rows, size), lambda d: (d, piece, 0))
    return pl.pallas_call(
        inter_kernel,
        grid=(loaders // group,),
        in_specs=[
            pl.BlockSpec(memory_space=pltpu.SMEM),
            pl.BlockSpec(memory_space=pltpu.SMEM),
            pl.BlockSpec((group, 1, rows, size), lambda d: (d, 0, piece, 0)),
            block,
            block,
            pl.BlockSpec((group, wide, size), lambda d: (d, 0, 0)),
            pl.BlockSpec((wide, size), lambda d: (0, 0)),
        ],
        out_specs=pl.BlockSpec((group, rows, size), lambda d: (d, 0, 0)),
        out_shape=jax.ShapeDtypeStruct((loaders, rows, size), bf16),
        scratch_shapes=[pltpu.VMEM((group, wide, size), bf16), pltpu.VMEM((group, rows, wide), bf16)],
        compiler_params=params(48, ("arbitrary",)),
        cost_estimate=tiny,
        name="inter",
    )(rate.reshape(1), decay, query_in, dest_wide, slot_wide, prefix, state)


def finish_kernel(inter_low, inter_high, intra_low, intra_high, gain_ref, *rest):
    out_ref, mixed = rest[-2:]
    heads, rows, size = intra_low.shape
    square = jnp.zeros((rows, size), f32)
    for half, (inter_ref, intra_ref) in enumerate(((inter_low, intra_low), (inter_high, intra_high))):
        for h in range(heads):
            value = intra_ref[h] + inter_ref[h].astype(f32)
            mixed[half * heads + h] = value
            square = square + value * value
    mean_square = jnp.sum(square, axis=1, keepdims=True) / (2 * heads * size)
    factor = lax.rsqrt(mean_square + eps_norm)
    normed = (mixed[...] * factor[None]) * gain_ref[...]
    out_ref[...] = jnp.swapaxes(normed.astype(bf16), 0, 1)


def finish(low_back, high_back, intra_terms, gain, piece, before):
    heads, all_rows, size = intra_terms[0].shape
    rows = 64
    steps = high_back.shape[1] // rows
    shift = piece * steps
    here = pl.BlockSpec((heads, rows, size), lambda i: (0, i + shift, 0))
    extra = [] if before is None else [before]
    return pl.pallas_call(
        finish_kernel,
        grid=(steps,),
        in_specs=[
            here,
            pl.BlockSpec((heads, rows, size), lambda i: (0, i, 0)),
            here,
            here,
            pl.BlockSpec((2 * heads, 1, size), lambda i: (0, 0, 0)),
        ]
        + [pl.BlockSpec(memory_space=pl.ANY)] * len(extra),
        out_specs=pl.BlockSpec((rows, 2 * heads, size), lambda i: (i + shift, 0, 0)),
        out_shape=jax.ShapeDtypeStruct((all_rows, 2 * heads, size), bf16),
        scratch_shapes=[pltpu.VMEM((2 * heads, rows, size), f32)],
        input_output_aliases={5: 0} if extra else {},
        compiler_params=params(60, ("arbitrary",)),
        cost_estimate=tiny,
        name="finish",
    )(low_back, high_back, *intra_terms, gain, *extra)


def swap(block, distance):
    count = lax.axis_size("seq")
    route = [(i, i + distance) for i in range(count) if i + distance < count]
    return lax.ppermute(block, "seq", route)


def other_core(block):
    return lax.ppermute(block, "seq", [(i, i ^ 1) for i in range(lax.axis_size("seq"))])


def incoming_states(total, counts, starts, rate):
    all_sequences = counts.shape[0]
    sequences = all_sequences // 2
    shard = lax.axis_index("seq")
    even = shard % 2 == 0
    wide, size = total.shape
    part = wide // 2
    chips = lax.axis_size("seq") // 2

    def decay(count, start):
        factor = jnp.where(start == 0.0, jnp.exp(-rate * count), 0.0)
        return jnp.broadcast_to(factor[:, None, None], (sequences, size, 1)).reshape(part, 1)

    def halves(numbers):
        return numbers[:sequences], numbers[sequences:]

    def lines(numbers, height, dtype):
        row = jnp.concatenate(numbers)
        row = jnp.pad(row, (0, size - row.shape[0]))
        return jnp.pad(row[None], ((0, height - 1), (0, 0))).astype(dtype)

    own = jnp.where(even, total[:part], total[part:])
    theirs = jnp.where(even, total[part:], total[:part])
    arrived = other_core(jnp.concatenate([theirs, lines([counts, starts], 8, f32)]))
    total_even = jnp.where(even, own, arrived[:part])
    total_odd = jnp.where(even, arrived[:part], own)
    facts = arrived[part]
    counts_low, counts_high = halves(counts)
    starts_low, starts_high = halves(starts)
    other_low, other_high = halves(facts[:all_sequences])
    begun_low, begun_high = halves(facts[all_sequences : 2 * all_sequences])
    counts_own = jnp.where(even, counts_low, counts_high)
    starts_own = jnp.where(even, starts_low, starts_high)
    counts_other = jnp.where(even, other_low, other_high)
    starts_other = jnp.where(even, begun_low, begun_high)
    decay_even = decay(jnp.where(even, counts_own, counts_other), jnp.where(even, starts_own, starts_other))
    decay_odd = decay(jnp.where(even, counts_other, counts_own), jnp.where(even, starts_other, starts_own))

    chip_count = counts_own + counts_other
    chip_start = jnp.minimum(starts_own + starts_other, 1.0)
    high = jnp.floor(chip_count / 128.0)
    packed = jnp.concatenate(
        [
            (decay_odd * total_even + total_odd).astype(bf16),
            lines([high, chip_count - 128.0 * high, chip_start], 16, bf16),
        ]
    )
    base = jnp.zeros_like(total_even)
    passed_count = jnp.zeros_like(chip_count)
    passed_start = jnp.zeros_like(chip_start)
    for distance in range(1, chips):
        earlier = swap(packed, 2 * distance)
        base = base + decay(passed_count, passed_start) * earlier[:part].astype(f32)
        row = earlier[part].astype(f32)
        passed_count = passed_count + 128.0 * row[:sequences] + row[sequences : 2 * sequences]
        passed_start = passed_start + row[2 * sequences : 3 * sequences]
    later = decay_even * base + total_even
    mine = jnp.where(even, base, later)
    got = other_core(jnp.where(even, later, base))
    return jnp.concatenate([jnp.where(even, mine, got), jnp.where(even, got, mine)])


def per_device(queries, key_rows, value_rows, destination, doc_starts, decay_rate, norm_gain):
    loaders = lax.axis_size("dp")
    rows, heads, size = queries.shape[2:]
    extra = 16
    lines = rows // size

    def exchange(block):
        return lax.all_to_all(block, "dp", split_axis=0, concat_axis=0, tiled=True)

    def after(block, *others):
        return lax.optimization_barrier((block,) + others)[0]

    dest = destination[0, 0]
    start = doc_starts[0, 0]
    sequence_ids = jnp.arange(loaders, dtype=jnp.int32)
    onehot = (dest[:, None] == sequence_ids[None, :]).astype(jnp.int32)
    both = jnp.concatenate([onehot, onehot * start[:, None]], axis=1)
    row_ids = jnp.arange(rows, dtype=jnp.int32)
    causal = row_ids[:, None] >= row_ids[None, :]
    summed = jnp.dot(causal.astype(bf16), both.astype(bf16), preferred_element_type=f32)

    onehot_f = onehot.astype(f32)
    counts = summed[:, :loaders]
    docs = summed[:, loaders:]
    slot = jnp.sum(counts * onehot_f, axis=1)
    doc = jnp.sum(docs * onehot_f, axis=1)
    last_count = jnp.sum(counts[-1:] * onehot_f, axis=1)
    last_doc = jnp.sum(docs[-1:] * onehot_f, axis=1)
    gap = jnp.where(doc == last_doc, last_count - slot, -1.0)
    gap_wide = jnp.broadcast_to(gap[:, None], (rows, size))
    info = jnp.concatenate(
        [
            dest.astype(bf16).reshape(lines, size),
            jnp.where(doc == 0, slot, 0.0).astype(bf16).reshape(lines, size),
            jnp.pad(summed[-1:].astype(bf16), ((0, extra - 2 * lines - 1), (0, size - 2 * loaders))),
        ]
    )

    keys_here, values_here = key_rows[0, 0], value_rows[0, 0]
    sent, keys_t, queries_t = [], [], []
    for half in range(2):
        send, key_t = prepare(decay_rate, keys_here, values_here, gap_wide, half, None if half else info)
        sent.append(send)
        keys_t.append(key_t)
        here = slice(half * loaders, (half + 1) * loaders)
        queries_t.append(jnp.transpose(queries[0, 0, :, here], (1, 0, 2))[:, None])
    first_in = exchange(sent[0])

    label = dest * rows + doc.astype(jnp.int32)
    mask = (causal & (label[:, None] == label[None, :])).astype(f32)
    col_scale = jnp.exp(decay_rate[:, None] * slot[None])[:, None]
    slot_here = jnp.broadcast_to(slot[:, None], (rows, size))
    intra_terms = [
        intra(decay_rate, queries_t[half], keys_t[half], sent[half], col_scale, mask, slot_here, half)
        for half in range(2)
    ]
    first_query = exchange(after(queries_t[0], first_in, *intra_terms))

    info_all = first_in[:, 0, rows:]
    dest_all = info_all[:, :lines].reshape(loaders, rows)
    slot_all = info_all[:, lines : 2 * lines].reshape(loaders, rows)
    count_all = info_all[:, 2 * lines, :loaders].astype(f32)
    start_all = info_all[:, 2 * lines, loaders : 2 * loaders].astype(f32)
    dest_wide = jnp.broadcast_to(dest_all[:, :, None], (loaders, rows, size))
    slot_wide = jnp.broadcast_to(slot_all[:, :, None], (loaders, rows, size))
    place = lax.axis_index("dp")
    rates = [decay_rate[place], decay_rate[loaders + place]]
    shard_counts = jnp.sum(count_all, axis=0)
    shard_starts = jnp.sum(start_all, axis=0)
    earlier = (sequence_ids[:, None] > sequence_ids[None, :]).astype(f32)[:, :, None]
    count_before = jnp.sum(earlier * count_all[None], axis=1)
    start_before = jnp.sum(earlier * start_all[None], axis=1)
    chunk_decays = [jnp.where(start_all == 0, jnp.exp(-rate * count_all), 0.0) for rate in rates]
    entry_decays = [jnp.where(start_before == 0, jnp.exp(-rate * count_before), 0.0) for rate in rates]

    prefix, total = update_states(chunk_decays[0], first_in, dest_all[:, None])
    second_in = exchange(after(sent[1], first_query, total))
    state = incoming_states(total, shard_counts, shard_starts, rates[0])
    low = inter(rates[0], entry_decays[0], first_query, dest_wide, slot_wide, prefix, state, 0, 1)

    second_in = after(second_in, low)
    second_query = exchange(after(queries_t[1], second_in))
    prefix, total = update_states(chunk_decays[1], second_in, dest_all[:, None])
    low_back = exchange(after(low, second_query))
    state = incoming_states(after(total, second_query), shard_counts, shard_starts, rates[1])
    pieces = 2
    high_backs = []
    arrived = low_back
    for piece in range(pieces):
        high = inter(
            rates[1], entry_decays[1], second_query, dest_wide, slot_wide, prefix, state, piece, pieces
        )
        arrived = exchange(after(high, arrived))
        high_backs.append(arrived)
    result = None
    for piece in range(pieces):
        result = finish(low_back, high_backs[piece], intra_terms, norm_gain[:, None], piece, result)
    return result[None, None]


def solution(mesh):
    placed = (
        P("dp", "seq", None, None, None),
        P("dp", "seq", None, None, None),
        P("dp", "seq", None, None, None),
        P("dp", "seq", None),
        P("dp", "seq", None),
        P(),
        P(),
    )
    return jax.shard_map(
        per_device,
        mesh=mesh,
        in_specs=placed,
        out_specs=P("dp", "seq", None, None, None),
        check_vma=False,
    )
```
